512 devices in a mesh: dp: 32 (over z, y_hi, core), tensor: 16 (over y_lo, x).
Axes of the slice: x: 4, y: 8 (y_hi: 2, y_lo: 4; y = y_hi * 4 + y_lo), z: 8, core: 2. Of those that a mesh axis runs over, the one named last changes fastest.
Arguments:
- features: bfloat16 [4096, 24576], P('tensor', 'dp'), may hold values from -6 to 6
- cotangent: bfloat16 [4096, 24576], P('tensor', 'dp'), may hold values from -6 to 6
- up_blocks: bfloat16 [16, 256, 1024], P('tensor'), may hold values from -0.375 to 0.375
- down_blocks: bfloat16 [16, 1024, 256], P('tensor'), may hold values from -0.1875 to 0.1875
Outputs:
- outputs: bfloat16 [4096, 24576], P('tensor', 'dp')
- feature_grads: bfloat16 [4096, 24576], P('tensor', 'dp')
- up_grads: float32 [16, 256, 1024], P('tensor', 'dp')
- down_grads: float32 [16, 1024, 256], P('tensor', 'dp')
The draws below stay inside these ranges and needn't reach their ends.
All inputs are finite; a program needn't handle non-finite values.
Results may differ from the reference program's by a relative error of at most 0.015.
Values may be sent and summed in bfloat16 or wider, within the bound.
A program may use at most 64 MiB of HBM per device.

```python
import math
import jax
import jax.numpy as jnp
from jax import lax

D = 4096
BLOCKS = 16
TOK_DEV = 768
TOKENS = 24576
DB = 256
FB = 1024
SUB = 64
N_DP = 32


def steps_of(key, dims, cuts, least, top_value):
    gain = 1.0
    for axis_at, parts in cuts:
        heights = jax.random.uniform(jax.random.fold_in(jax.random.fold_in(key, 6), axis_at), (parts,), jnp.float32, least / len(cuts), top_value / len(cuts))
        gain = gain * jnp.repeat(jnp.exp(heights), dims[axis_at] // parts).reshape((-1,) + (1,) * (len(dims) - 1 - axis_at))
    return gain


def normal_values(rng, shape, width, bound, shards=(), kind=jnp.bfloat16):
    loudness = steps_of(rng, shape, shards, -0.22, 0.18) if shards else 1.0
    entries = jax.random.normal(rng, shape, jnp.float32) * width * loudness
    return jnp.minimum(jnp.maximum(entries, -bound), bound).astype(kind)


def setup_inputs(seed: int = 0) -> dict:
    keys = jax.random.split(jax.random.key(seed), 5)
    features = normal_values(keys[0], (D, TOKENS), 1.0, 6.0, ((0, 16), (1, 32)))
    cotangent = normal_values(keys[1], (D, TOKENS), 1.0, 6.0, ((0, 16), (1, 32)))
    up_blocks = normal_values(keys[2], (BLOCKS, DB, FB), DB ** -0.5, 0.375, ((0, 16),))
    down_blocks = normal_values(keys[3], (BLOCKS, FB, DB), FB ** -0.5, 0.1875, ((0, 16),))
    return dict(features=features, cotangent=cotangent, up_blocks=up_blocks, down_blocks=down_blocks)


INV_ROOT2 = 0.7071067811865476
INV_ROOT2PI = 0.3989422804014327

def gelu_value(value):
    return 0.5 * value * (1.0 + lax.erf(value * INV_ROOT2))

def gelu_slope(value):
    return 0.5 * (1.0 + lax.erf(value * INV_ROOT2)) + value * jnp.exp(-0.5 * value * value) * INV_ROOT2PI

def rounded(value):
    return lax.optimization_barrier(value.astype(jnp.bfloat16)).astype(jnp.float32)

def reference(features, cotangent, up_blocks, down_blocks):
    up_wide = up_blocks.astype(jnp.float32)
    down_wide = down_blocks.astype(jnp.float32).reshape(BLOCKS, BLOCKS, SUB, DB)

    def step(carry, index):
        grad_up, grad_down = carry
        begin = (index * TOK_DEV).astype(jnp.int32)
        x_block = lax.dynamic_slice_in_dim(features, begin, TOK_DEV, 1).astype(jnp.float32).reshape(BLOCKS, DB, TOK_DEV)
        dy_block = lax.dynamic_slice_in_dim(cotangent, begin, TOK_DEV, 1).astype(jnp.float32).reshape(BLOCKS, DB, TOK_DEV)
        preact = rounded(jnp.einsum('bdn,bdf->bfn', x_block, up_wide))
        hidden = rounded(gelu_value(preact)).reshape(BLOCKS, BLOCKS, SUB, TOK_DEV)
        out_block = jnp.einsum('ijsn,jise->jen', hidden, down_wide).astype(jnp.bfloat16).reshape(D, TOK_DEV)
        back = rounded(jnp.einsum('jen,jise->ijsn', dy_block, down_wide)).reshape(BLOCKS, FB, TOK_DEV)
        slope = rounded(back * gelu_slope(preact))
        dx_block = jnp.einsum('bfn,bdf->bdn', slope, up_wide).astype(jnp.bfloat16).reshape(D, TOK_DEV)
        grad_up = grad_up + jnp.einsum('bdn,bfn->bdf', x_block, slope)
        grad_down = grad_down + jnp.einsum('ijsn,jen->jise', hidden, dy_block).reshape(BLOCKS, FB, DB)
        return ((grad_up, grad_down), (out_block, dx_block))
    start_up = jnp.zeros((BLOCKS, DB, FB), jnp.float32)
    start_down = jnp.zeros((BLOCKS, FB, DB), jnp.float32)
    (grad_up, grad_down), (outs, dxs) = lax.scan(step, (start_up, start_down), jnp.arange(N_DP, dtype=jnp.int32))
    outputs = jnp.transpose(outs, (1, 0, 2)).reshape(D, TOKENS)
    feature_grads = jnp.transpose(dxs, (1, 0, 2)).reshape(D, TOKENS)
    factor = 1.0 / math.sqrt(TOKENS)
    return (outputs, feature_grads, grad_up * factor, grad_down * factor)
```

```python
import math

import jax
import jax.numpy as jnp
from jax import lax
from jax.sharding import PartitionSpec as P

BLOCKS = 16
SUB = 64


INV_ROOT2 = 0.7071067811865476
INV_ROOT2PI = 0.3989422804014327


def gelu_value(value):
    return 0.5 * value * (1.0 + lax.erf(value * INV_ROOT2))


def gelu_slope(value):
    return (
        0.5 * (1.0 + lax.erf(value * INV_ROOT2))
        + value * jnp.exp(-0.5 * value * value) * INV_ROOT2PI
    )


def on_device(features, cotangent, up_blocks, down_blocks):
    local_blocks = up_blocks.shape[0]
    block_feat = up_blocks.shape[1]
    block_hidden = up_blocks.shape[2]
    tokens_here = features.shape[1]
    n_dp = lax.axis_size("dp")
    factor = 1.0 / math.sqrt(tokens_here * n_dp)
    x_local = features.reshape(local_blocks, block_feat, tokens_here)
    dy_local = cotangent.reshape(local_blocks, block_feat, tokens_here)
    down_four = down_blocks.reshape(local_blocks, BLOCKS, SUB, block_feat)
    preact = jnp.einsum(
        "bdn,bdf->bfn", x_local, up_blocks, preferred_element_type=jnp.float32
    ).astype(jnp.bfloat16)
    pre_wide = preact.astype(jnp.float32)
    hidden = (
        gelu_value(pre_wide).astype(jnp.bfloat16).reshape(local_blocks, BLOCKS, SUB, tokens_here)
    )
    mixed = lax.all_to_all(hidden, "tensor", split_axis=1, concat_axis=0, tiled=True)
    out_three = jnp.einsum(
        "ijsn,jise->jen", mixed, down_four, preferred_element_type=jnp.float32
    ).astype(jnp.bfloat16)
    outputs = out_three.reshape(local_blocks * block_feat, tokens_here)
    down_term = jnp.einsum("ijsn,jen->isje", mixed, dy_local, preferred_element_type=jnp.float32)
    down_term = down_term.reshape(block_hidden, local_blocks, block_feat)
    back = jnp.einsum(
        "jen,jise->ijsn", dy_local, down_four, preferred_element_type=jnp.float32
    ).astype(jnp.bfloat16)
    back_home = lax.all_to_all(back, "tensor", split_axis=0, concat_axis=1, tiled=True)
    back_home = back_home.reshape(local_blocks, block_hidden, tokens_here)
    slope = (back_home.astype(jnp.float32) * gelu_slope(pre_wide)).astype(jnp.bfloat16)
    up_term = jnp.einsum("bdn,bfn->dbf", x_local, slope, preferred_element_type=jnp.float32)
    dx_three = jnp.einsum(
        "bfn,bdf->bdn", slope, up_blocks, preferred_element_type=jnp.float32
    ).astype(jnp.bfloat16)
    feature_grads = dx_three.reshape(local_blocks * block_feat, tokens_here)
    terms = jnp.concatenate(
        [
            up_term.astype(jnp.bfloat16).reshape(n_dp, -1, 128),
            down_term.astype(jnp.bfloat16).reshape(n_dp, -1, 128),
        ],
        axis=1,
    )
    shares = lax.all_to_all(terms, "dp", split_axis=0, concat_axis=0, tiled=True)
    total = jnp.sum(shares.astype(jnp.float32), axis=0) * factor
    half = total.shape[0] // 2
    up_grads = total[:half].reshape(local_blocks, block_feat // n_dp, block_hidden)
    down_grads = total[half:].reshape(local_blocks, block_hidden // n_dp, block_feat)
    return (outputs, feature_grads, up_grads, down_grads)


def solution(mesh):
    in_specs = (
        P("tensor", "dp"),
        P("tensor", "dp"),
        P("tensor", None, None),
        P("tensor", None, None),
    )
    out_specs = (
        P("tensor", "dp"),
        P("tensor", "dp"),
        P("tensor", "dp", None),
        P("tensor", "dp", None),
    )
    return jax.shard_map(
        on_device, mesh=mesh, in_specs=in_specs, out_specs=out_specs, check_vma=False
    )
```

```python
import math

import jax
import jax.numpy as jnp
from jax import lax
from jax.experimental import pallas as pl
from jax.experimental.pallas import tpu as pltpu
from jax.sharding import PartitionSpec as P

LINE = 4
RING = 4
SUB = 64
CHUNKS = 3
OWNERS = 16

INV_ROOT2 = 0.7071067811865476
INV_ROOT2PI = 0.3989422804014327

BF16 = jnp.bfloat16
F32 = jnp.float32
MESH = pl.DeviceIdType.MESH


def dot(a, b):
    return jnp.dot(a, b, preferred_element_type=F32)


def dot_nt(a, b):
    return lax.dot_general(a, b, (((1,), (1,)), ((), ())), preferred_element_type=F32)


def kernel(
    x_hbm, dy_hbm, up_hbm, down_hbm,
    out_ref, dx_ref, upg_ref, downg_ref,
    xc, dy, upv, upt, dw, dwt, hs, h, sf, b, g, rss, rsr,
    dacc, uacc, ds, dr, dz, dq, dfin, dgot, us, ur, uz, uq,
    load_sem, w_send, w_recv, ag_send, ag_recv, hs_send, hs_recv, h_loc, b_send, b_recv, b_loc,
    rs_send, rs_recv, dc_sem, dz_send, dz_recv, df_sem, uc_sem, uz_send, uz_recv,
):
    chunks, wide, tc = xc.shape
    dp = lax.axis_index("dp")
    tensor = lax.axis_index("tensor")
    z = dp // 4
    yh = (dp // 2) % 2
    core = dp % 2
    yl = tensor // 4
    x = tensor % 4
    y8 = yh * 4 + yl
    me = dp // 2
    interior = jnp.logical_and(yl > 0, yl < LINE - 1)

    def at_y(delta):
        to = (y8 + delta + 8) % 8
        return {"dp": (z * 2 + to // 4) * 2 + core, "tensor": (to % 4) * 4 + x}

    def at_line(to):
        return {"dp": dp, "tensor": to * 4 + x}

    def at_x(to):
        return {"dp": dp, "tensor": yl * 4 + to}

    def at_owner(o):
        return {"dp": o * 2 + core, "tensor": tensor}

    other_core = {"dp": dp + 1 - 2 * core, "tensor": tensor}
    swap_y = z // 2
    swap = {"dp": ((2 * yl + z % 2) * 2 + yh) * 2 + core, "tensor": swap_y * 4 + x}
    swaps = swap_y != yl

    def remote(src, dst, send, recv, where):
        return pltpu.make_async_remote_copy(
            src_ref=src, dst_ref=dst, send_sem=send, recv_sem=recv, device_id=where, device_id_type=MESH
        )

    barrier = pltpu.get_barrier_semaphore()

    def greet(where):
        pl.semaphore_signal(barrier, inc=1, device_id=where, device_id_type=MESH)

    for delta in (1, -1, 2, -2):
        greet(at_y(delta))
    for k in range(1, RING):
        greet(at_x((x + k) % RING))
    greet(other_core)
    for k in range(1, OWNERS):
        greet(at_owner((me + k) % OWNERS))

    @pl.when(swaps)
    def _():
        greet(swap)

    up_load = pltpu.make_async_copy(up_hbm.at[0], upv, load_sem.at[0])
    up_load.start()
    x_loads = []
    dy_loads = []
    for c in range(chunks):
        cp = pltpu.make_async_copy(x_hbm.at[:, pl.ds(c * tc, tc)], xc.at[c], load_sem.at[1 + c])
        cp.start()
        x_loads.append(cp)
    for c in range(chunks):
        cp = pltpu.make_async_copy(dy_hbm.at[:, pl.ds(c * tc, tc)], dy.at[yl, c], load_sem.at[1 + chunks + c])
        cp.start()
        dy_loads.append(cp)
    dw_load = pltpu.make_async_copy(
        down_hbm.at[0, pl.ds(yl * 256, 256)], dw.at[yl], load_sem.at[1 + 2 * chunks]
    )
    dw_load.start()

    sends = []

    def hidden(c):
        def body(k, carry):
            p = dot(upt[pl.ds(k * 256, 256), :], xc[c]).astype(BF16).astype(F32)
            cdf = 0.5 * (1.0 + lax.erf(p * INV_ROOT2))
            hs[c, k] = (p * cdf).astype(BF16).reshape(RING, SUB, tc)
            sf[c, pl.ds(k * 256, 256), :] = cdf + p * jnp.exp(-0.5 * p * p) * INV_ROOT2PI
            return carry

        lax.fori_loop(0, LINE, body, 0)

    def send_hidden(c):
        own = pltpu.make_async_copy(hs.at[c, :, x], h.at[c, :, x], h_loc.at[c])
        own.start()
        for k in range(1, RING):
            to = (x + k) % RING
            cp = remote(hs.at[c, :, to], h.at[c, :, x], hs_send.at[c, k - 1], hs_recv.at[c, k - 1], at_x(to))
            cp.start()
            sends.append(cp)

    def wait_hidden(c):
        pltpu.make_async_copy(hs.at[c, :, x], h.at[c, :, x], h_loc.at[c]).wait()
        for k in range(1, RING):
            fr = (x - k + RING) % RING
            remote(hs.at[c, :, fr], h.at[c, :, fr], hs_send.at[c, k - 1], hs_recv.at[c, k - 1], at_x(fr)).wait_recv()

    near = [yl + 1 - 2 * (yl % 2), 2 - yl // 2, 3 - 3 * (yl // 2)]

    def gather(c, k):
        s = near[k]
        to = jnp.where(s > yl, yl - 1, yl + 1)
        cp = remote(dy.at[s, c], dy.at[s, c], ag_send.at[2 + k, c], ag_recv.at[s, c], at_line(to))
        cp.wait_recv()

        @pl.when(interior)
        def _():
            cp.start()

    def gather_end(c, k):
        s = near[k]

        @pl.when(interior)
        def _():
            remote(dy.at[s, c], dy.at[s, c], ag_send.at[2 + k, c], ag_recv.at[s, c], at_line(yl)).wait_send()

    def send_back(c):
        def body(s, carry):
            b[c, s] = dot(dw[s], dy[s, c]).astype(BF16).reshape(RING, SUB, tc)
            return carry

        lax.fori_loop(0, LINE, body, 0)
        own = pltpu.make_async_copy(b.at[c, :, x], g.at[c, :, x], b_loc.at[c])
        own.start()
        for k in range(1, RING):
            to = (x + k) % RING
            cp = remote(b.at[c, :, to], g.at[c, :, x], b_send.at[c, k - 1], b_recv.at[c, k - 1], at_x(to))
            cp.start()
            sends.append(cp)

    def wait_back(c):
        pltpu.make_async_copy(b.at[c, :, x], g.at[c, :, x], b_loc.at[c]).wait()
        for k in range(1, RING):
            fr = (x - k + RING) % RING
            remote(b.at[c, :, fr], g.at[c, :, fr], b_send.at[c, k - 1], b_recv.at[c, k - 1], at_x(fr)).wait_recv()

    def partial(c, s):
        return dot(dwt[s], h[c, s].reshape(256, tc))

    def pass_outputs(c):
        for k in range(LINE - 1):
            s = near[LINE - 2 - k]
            above = s > yl
            to = jnp.where(above, yl + 1, yl - 1)

            @pl.when(jnp.logical_not(interior))
            def _():
                rss[c, s] = partial(c, s).astype(BF16)

            @pl.when(interior)
            def _():
                remote(rss.at[c, s], rsr.at[c, s], rs_send.at[c, k], rs_recv.at[c, s], at_line(yl)).wait_recv()
                rss[c, s] = (partial(c, s) + rsr[c, s].astype(F32)).astype(BF16)

            slot = jnp.where(jnp.logical_and(to == s, above), LINE, s)
            cp = remote(rss.at[c, s], rsr.at[c, slot], rs_send.at[c, k], rs_recv.at[c, slot], at_line(to))
            cp.start()
            sends.append(cp)

    def end_outputs(c):
        mine = pl.ds(c * tc, tc)
        total = partial(c, yl)

        @pl.when(yl == 0)
        def _():
            remote(rss.at[c, 0], rsr.at[c, 0], rs_send.at[c, 0], rs_recv.at[c, 0], at_line(yl)).wait_recv()
            out_ref[:, mine] = (total + rsr[c, 0].astype(F32)).astype(BF16)

        @pl.when(yl == LINE - 1)
        def _():
            remote(rss.at[c, 0], rsr.at[c, LINE], rs_send.at[c, 0], rs_recv.at[c, LINE], at_line(yl)).wait_recv()
            out_ref[:, mine] = (total + rsr[c, LINE].astype(F32)).astype(BF16)

        @pl.when(interior)
        def _():
            remote(rss.at[c, 0], rsr.at[c, yl], rs_send.at[c, 0], rs_recv.at[c, yl], at_line(yl)).wait_recv()
            remote(rss.at[c, 0], rsr.at[c, LINE], rs_send.at[c, 0], rs_recv.at[c, LINE], at_line(yl)).wait_recv()
            out_ref[:, mine] = (total + rsr[c, yl].astype(F32) + rsr[c, LINE].astype(F32)).astype(BF16)

    def down_term(c):
        def body(s, carry):
            term = dot_nt(h[c, s].reshape(256, tc), dy[s, c])
            if c == 0:
                dacc[s] = term
            else:
                dacc[s] += term
            return carry

        lax.fori_loop(0, LINE, body, 0)

    def slope_step(c):
        wait_back(c)

        def body(k, carry):
            rows = pl.ds(k * 256, 256)
            back = g[c, k].reshape(256, tc).astype(F32)
            slope = (back * sf[c, rows, :]).astype(BF16)
            g[c, k] = slope.reshape(RING, SUB, tc)
            term = dot_nt(xc[c], slope)
            if c == 0:
                uacc[k] = term
            else:
                uacc[k] += term
            return carry

        lax.fori_loop(0, LINE, body, 0)

    def feature_step(c):
        dx_ref[:, pl.ds(c * tc, tc)] = dot(upv[...], g[c].reshape(1024, tc)).astype(BF16)

    up_load.wait()
    upt[...] = upv[...].T
    x_loads[0].wait()
    hidden(0)
    for cp in dy_loads:
        cp.wait()
    dw_load.wait()

    pl.semaphore_wait(barrier, 23 + jnp.where(swaps, 1, 0))

    def send_dy(c, start):
        for way, ok in ((1, yl < LINE - 1), (-1, yl > 0)):

            @pl.when(ok)
            def _():
                cp = remote(
                    dy.at[yl, c], dy.at[yl, c], ag_send.at[(1 - way) // 2, c], ag_recv.at[yl, c], at_line(yl + way)
                )
                if start:
                    cp.start()
                else:
                    cp.wait_send()

    send_dy(0, True)
    send_hidden(0)
    far = 2 - 4 * core
    w_copies = []
    for k, delta in enumerate((1, -1, far)):
        to = (y8 + delta + 8) % 8
        cp = remote(
            down_hbm.at[0, pl.ds((to % 4) * 256, 256)], dw.at[yl], w_send.at[k], w_recv.at[yl], at_y(delta)
        )
        cp.start()
        w_copies.append(cp)
    for c in range(1, chunks):
        send_dy(c, True)

    dwt[yl] = dw[yl].T
    for c in range(1, chunks):
        x_loads[c].wait()
        hidden(c)
        send_hidden(c)
        gather(c - 1, 0)
    for k in range(1, LINE):
        s = (yl + k) % LINE
        remote(dw.at[s], dw.at[s], w_send.at[0], w_recv.at[s], at_line(yl)).wait_recv()
        dwt[s] = dw[s].T
    for c in range(chunks):
        if c == chunks - 1:
            gather(c, 0)
        gather(c, 1)
        gather(c, 2)
        send_back(c)
        wait_hidden(c)
        pass_outputs(c)
        down_term(c)

    def split(s, carry):
        for i in range(RING):
            for half in range(2):
                ds[half, s * RING + i] = dacc[s, pl.ds(i * 64 + half * 32, 32), :].astype(BF16)
        return carry

    lax.fori_loop(0, LINE, split, 0)
    dc = remote(ds.at[1 - core], dr, dc_sem.at[0], dc_sem.at[1], other_core)
    dc.start()
    end_outputs(0)
    slope_step(0)
    dc.wait()

    def join(s, carry):
        for i in range(RING):
            mine = dacc[s, pl.ds(pl.multiple_of(i * 64 + core * 32, 32), 32), :]
            dz[s * RING + i] = (mine + dr[s * RING + i].astype(F32)).astype(BF16)
        return carry

    lax.fori_loop(0, LINE, join, 0)
    for k in range(1, OWNERS):
        o = (me + k) % OWNERS
        cp = remote(dz.at[o], dq.at[me], dz_send.at[k - 1], dz_recv.at[k - 1], at_owner(o))
        cp.start()
        sends.append(cp)
    feature_step(0)
    end_outputs(1)
    slope_step(1)
    feature_step(1)
    factor = 1.0 / math.sqrt(tc * chunks * 32)
    total = dz[me].astype(F32)
    for k in range(1, OWNERS):
        fr = (me - k + OWNERS) % OWNERS
        remote(dz.at[fr], dq.at[fr], dz_send.at[k - 1], dz_recv.at[k - 1], at_owner(fr)).wait_recv()
        total += dq[fr].astype(F32)
    dfin[...] = total * factor

    @pl.when(swaps)
    def _():
        remote(dfin, dgot, df_sem.at[0], df_sem.at[1], swap).start()

    slope_step(2)

    def split_up(o, carry):
        for half in range(2):
            rows = pl.ds(pl.multiple_of(16 * o + 8 * half, 8), 8)
            low = jnp.concatenate([uacc[0, rows, :], uacc[1, rows, :]], axis=1)
            high = jnp.concatenate([uacc[2, rows, :], uacc[3, rows, :]], axis=1)
            us[half, o] = jnp.concatenate([low, high], axis=0).astype(BF16)
        return carry

    lax.fori_loop(0, OWNERS, split_up, 0)
    uc = remote(us.at[1 - core], ur, uc_sem.at[0], uc_sem.at[1], other_core)
    uc.start()
    feature_step(2)
    uc.wait()

    def join_up(o, carry):
        uz[o] = (us[core, o].astype(F32) + ur[o].astype(F32)).astype(BF16)
        return carry

    lax.fori_loop(0, OWNERS, join_up, 0)
    for k in range(1, OWNERS):
        o = (me + k) % OWNERS
        cp = remote(uz.at[o], uq.at[me], uz_send.at[k - 1], uz_recv.at[k - 1], at_owner(o))
        cp.start()
        sends.append(cp)
    end_outputs(2)

    @pl.when(swaps)
    def _():
        remote(dfin, dgot, df_sem.at[0], df_sem.at[1], swap).wait()
        downg_ref[0] = dgot[...]

    @pl.when(jnp.logical_not(swaps))
    def _():
        downg_ref[0] = dfin[...]

    total = uz[me].astype(F32)
    for k in range(1, OWNERS):
        fr = (me - k + OWNERS) % OWNERS
        remote(uz.at[fr], uq.at[fr], uz_send.at[k - 1], uz_recv.at[k - 1], at_owner(fr)).wait_recv()
        total += uq[fr].astype(F32)
    total = total * factor
    upg_ref[0, :, pl.ds(0, 512)] = total[:8]
    upg_ref[0, :, pl.ds(512, 512)] = total[8:]

    for cp in sends:
        cp.wait_send()
    for cp in w_copies:
        cp.wait_send()
    for c in range(chunks):
        send_dy(c, False)
        for k in range(LINE - 1):
            gather_end(c, k)


def on_device(features, cotangent, up_blocks, down_blocks):
    wide, tokens = features.shape
    tc = tokens // CHUNKS
    hidden_units = up_blocks.shape[2]
    vm = pltpu.VMEM
    dma = pltpu.SemaphoreType.DMA
    grid = (CHUNKS, LINE, RING, SUB, tc)
    scratch = [
        vm((CHUNKS, wide, tc), BF16),
        vm((LINE, CHUNKS, wide, tc), BF16),
        vm((wide, hidden_units), BF16),
        vm((hidden_units, wide), BF16),
        vm((LINE, 256, wide), BF16),
        vm((LINE, wide, 256), BF16),
        vm(grid, BF16),
        vm(grid, BF16),
        vm((CHUNKS, hidden_units, tc), F32),
        vm(grid, BF16),
        vm(grid, BF16),
        vm((CHUNKS, LINE, wide, tc), BF16),
        vm((CHUNKS, LINE + 1, wide, tc), BF16),
        vm((LINE, 256, wide), F32),
        vm((LINE, wide, 256), F32),
        vm((2, OWNERS, 32, wide), BF16),
        vm((OWNERS, 32, wide), BF16),
        vm((OWNERS, 32, wide), BF16),
        vm((OWNERS, 32, wide), BF16),
        vm((32, wide), F32),
        vm((32, wide), F32),
        vm((2, OWNERS, 16, 512), BF16),
        vm((OWNERS, 16, 512), BF16),
        vm((OWNERS, 16, 512), BF16),
        vm((OWNERS, 16, 512), BF16),
        dma((2 + 2 * CHUNKS,)),
        dma((3,)), dma((LINE,)),
        dma((5, CHUNKS)), dma((LINE, CHUNKS)),
        dma((CHUNKS, 3)), dma((CHUNKS, 3)), dma((CHUNKS,)),
        dma((CHUNKS, 3)), dma((CHUNKS, 3)), dma((CHUNKS,)),
        dma((CHUNKS, 3)), dma((CHUNKS, LINE + 1)),
        dma((2,)), dma((OWNERS - 1,)), dma((OWNERS - 1,)), dma((2,)),
        dma((2,)), dma((OWNERS - 1,)), dma((OWNERS - 1,)),
    ]
    vmem = pl.BlockSpec(memory_space=pltpu.VMEM)
    hbm = pl.BlockSpec(memory_space=pl.ANY)
    return pl.pallas_call(
        kernel,
        name="monarch",
        out_shape=(
            jax.ShapeDtypeStruct((wide, tokens), BF16),
            jax.ShapeDtypeStruct((wide, tokens), BF16),
            jax.ShapeDtypeStruct((1, 8, hidden_units), F32),
            jax.ShapeDtypeStruct((1, 32, wide), F32),
        ),
        in_specs=[hbm] * 4,
        out_specs=[vmem] * 4,
        scratch_shapes=scratch,
        compiler_params=pltpu.CompilerParams(
            collective_id=0, has_side_effects=True, vmem_limit_bytes=50 * 2**20
        ),
    )(features, cotangent, up_blocks, down_blocks)


def solution(mesh):
    in_specs = (
        P("tensor", "dp"),
        P("tensor", "dp"),
        P("tensor", None, None),
        P("tensor", None, None),
    )
    out_specs = (
        P("tensor", "dp"),
        P("tensor", "dp"),
        P("tensor", "dp", None),
        P("tensor", "dp", None),
    )
    return jax.shard_map(
        on_device, mesh=mesh, in_specs=in_specs, out_specs=out_specs, check_vma=False
    )
```

```python
import math

import jax
import jax.numpy as jnp
from jax import lax
from jax.experimental import pallas as pl
from jax.experimental.pallas import tpu as pltpu
from jax.sharding import PartitionSpec as P

LINE = 4
RING = 4
SUB = 64
CHUNKS = 3
OWNERS = 16
Z = 8
SHARERS = 2

PLAN = (
    ("begin",), ("weights",), ("dy", 0, 1, 2), ("prepare_up",), ("hidden", 0), ("weights_pass",), ("prepare",),
    ("hidden", 1), ("i1", 0), ("i2", 0), ("b", 0, 1, 2), ("hidden", 2), ("weights_in",), ("i1", 1), ("i2", 1),
    ("hidden_in", 0), ("r1", 0), ("i1", 2), ("i2", 2), ("ib1", 0, 1, 2), ("e1", 0), ("eb1", 0), ("e1", 1),
    ("eb1", 1), ("e1", 2), ("eb1", 2), ("i3", 0), ("hidden_in", 1), ("r1", 1), ("i3", 1), ("r2", 0),
    ("ib2", 0, 1, 2), ("i3", 2), ("ib3", 0, 1, 2), ("e2", 0), ("eb2", 0), ("e2", 1), ("eb2", 1), ("e2", 2),
    ("eb2", 2), ("r3", 0), ("hidden_in", 2), ("r1", 2), ("down", 0, 1, 2), ("split0",), ("slope0", 0, 1, 2),
    ("r2", 1), ("join0",), ("slope1", 0, 1, 2), ("e3", 0), ("eb3", 0), ("e3", 1), ("eb3", 1), ("e3", 2),
    ("eb3", 2), ("down", 3), ("split2",), ("r3", 1), ("join2",), ("slope2", 0, 1, 2), ("split1",), ("sum0",),
    ("slope3", 0, 1, 2), ("split3",), ("join1",), ("end0",), ("out", 0), ("r2", 2), ("join3",), ("sum1",),
    ("end2",), ("out", 1), ("r3", 2), ("end1",), ("dx", 0, 1, 2), ("out", 2), ("end3",), ("down_end",),
)
GROUPS = (
    ((("down", 0), ("down", 1), ("down", 2),), False),
    ((("up", 0), ("up", 1), ("up", 2),), False),
    ((("down", 3),), True),
    ((("up", 3),), True),
)

INV_ROOT2 = 0.7071067811865476
INV_ROOT2PI = 0.3989422804014327

BF16 = jnp.bfloat16
F32 = jnp.float32
MESH = pl.DeviceIdType.MESH


def dot(a, b):
    return jnp.dot(a, b, preferred_element_type=F32)


def dot_nt(a, b):
    return lax.dot_general(a, b, (((1,), (1,)), ((), ())), preferred_element_type=F32)


def kernel(
    x_hbm, dy_hbm, up_hbm, down_hbm,
    out_ref, dx_ref, upg_ref, downg_ref,
    xc, dy, upv, upt, dw, dwt, hs, h, sf, b, g, rss, rsr,
    dacc, uacc, dfin, dgot,
    load_sem, w_send, w_recv, w2_recv, ag_send, ag_recv, hs_send, hs_recv, b_send, b_recv,
    rs_send, rs_recv, df_send, df_recv, *group_refs,
):
    chunks, wide, tc = xc.shape
    dp = lax.axis_index("dp")
    tensor = lax.axis_index("tensor")
    z = dp // 4
    yh = (dp // 2) % 2
    core = dp % 2
    yl = tensor // 4
    x = tensor % 4
    y8 = yh * 4 + yl
    me = dp // 2
    interior = jnp.logical_and(yl > 0, yl < LINE - 1)

    def at_y(delta):
        to = (y8 + delta + 8) % 8
        return {"dp": (z * 2 + to // 4) * 2 + core, "tensor": (to % 4) * 4 + x}

    def at_line(to):
        return {"dp": dp, "tensor": to * 4 + x}

    def at_x(to):
        return {"dp": dp, "tensor": yl * 4 + to}

    def at_owner(o):
        return {"dp": o * 2 + core, "tensor": tensor}

    part = (z % SHARERS) * 2 + core

    def at_sharer(p):
        return {"dp": ((z // SHARERS * SHARERS + p // 2) * 2 + yh) * 2 + p % 2, "tensor": tensor}

    other_core = {"dp": dp + 1 - 2 * core, "tensor": tensor}
    final_z = 2 * yl + z // 4
    final_yh = (z // 2) % 2
    stays = jnp.logical_and(final_z == z, final_yh == yh)
    piece = (z % 2) * 2 + yh

    def at_final(row):
        return {"dp": (final_z * 2 + final_yh) * 2 + core, "tensor": row * 4 + x}

    from_y = z // 2
    from_x = (z % 2) * 2 + yh

    def at_source(n):
        return {"dp": ((2 * from_x + n // 2) * 2 + n % 2) * 2 + core, "tensor": from_y * 4 + x}

    def is_self(n):
        same = jnp.logical_and(2 * from_x + n // 2 == z, n % 2 == yh)
        return jnp.logical_and(from_y == yl, same)

    def remote(src, dst, send, recv, where):
        return pltpu.make_async_remote_copy(
            src_ref=src, dst_ref=dst, send_sem=send, recv_sem=recv, device_id=where, device_id_type=MESH
        )

    barrier = pltpu.get_barrier_semaphore()

    def greet(where):
        pl.semaphore_signal(barrier, inc=1, device_id=where, device_id_type=MESH)

    for delta in (1, -1, 2, -2):
        greet(at_y(delta))
    for k in range(1, RING):
        greet(at_x((x + k) % RING))
    greet(other_core)
    for k in range(1, OWNERS):
        greet(at_owner((me + k) % OWNERS))

    for n in range(1, SHARERS):
        greet(at_sharer((part + 2 * n + 1 - 2 * core) % (2 * SHARERS)))
    for k in range(LINE):

        @pl.when(jnp.logical_not(jnp.logical_and(stays, k == yl)))
        def _():
            greet(at_final(k))

        @pl.when(jnp.logical_not(is_self(k)))
        def _():
            greet(at_source(k))

    up_load = pltpu.make_async_copy(up_hbm.at[0], upv, load_sem.at[0])
    up_load.start()
    x_loads = []
    for c in range(chunks):
        cp = pltpu.make_async_copy(x_hbm.at[:, pl.ds(c * tc, tc)], xc.at[c], load_sem.at[1 + c])
        cp.start()
        x_loads.append(cp)
    for c in range(chunks):
        cp = pltpu.make_async_copy(dy_hbm.at[:, pl.ds(c * tc, tc)], dy.at[yl, c], load_sem.at[1 + chunks])
        cp.start()
    dw_load = pltpu.make_async_copy(
        down_hbm.at[0, pl.ds(yl * 256, 256)], dw.at[yl], load_sem.at[2 + chunks]
    )
    dw_load.start()


    def hidden(c):
        def body(k, carry):
            p = dot(upt[pl.ds(k * 256, 256), :], xc[c]).astype(BF16).astype(F32)
            cdf = 0.5 * (1.0 + lax.erf(p * INV_ROOT2))
            hs[c, k] = (p * cdf).astype(BF16).reshape(RING, SUB, tc)
            sf[c, pl.ds(k * 256, 256), :] = cdf + p * jnp.exp(-0.5 * p * p) * INV_ROOT2PI
            return carry

        lax.fori_loop(0, LINE, body, 0)

    def send_hidden(c):
        for k in range(1, RING):
            to = (x + k) % RING
            cp = remote(hs.at[c, :, to], h.at[c, :, x], hs_send.at[0], hs_recv.at[c], at_x(to))
            cp.start()
        h[c, :, x] = hs[c, :, x]

    def wait_hidden(c):
        got = h.at[c, :, pl.ds(0, RING - 1)]
        remote(got, got, hs_send.at[0], hs_recv.at[c], at_x(x)).wait_recv()

    near = [yl + 1 - 2 * (yl % 2), 2 - yl // 2, 3 - 3 * (yl // 2)]

    edge = jnp.logical_not(interior)

    def gather(c, k, role):
        s = near[k]
        to = jnp.where(s > yl, yl - 1, yl + 1)

        @pl.when(role)
        def _():
            cp = remote(dy.at[s, c], dy.at[s, c], ag_send.at[2], ag_recv.at[s, c], at_line(to))
            cp.wait_recv()
            if role is interior:
                cp.start()

    order = [yl] + near

    def back_sends(c, k):
        s = order[k]
        copies = []
        for n in range(1, RING):
            to = (x + n) % RING
            copies.append(
                remote(b.at[c, s, to], g.at[c, s, x], b_send.at[0], b_recv.at[c, k], at_x(to))
            )
        return copies

    def send_back(c, k, role):
        def run():
            s = order[k]
            b[c, s] = dot(dw[s], dy[s, c]).astype(BF16).reshape(RING, SUB, tc)
            for cp in back_sends(c, k):
                cp.start()
            g[c, s, x] = b[c, s, x]

        if role is None:
            run()
        else:
            pl.when(role)(run)

    def wait_back(c, k):
        got = g.at[c, order[k], pl.ds(0, RING - 1)]
        remote(got, got, b_send.at[0], b_recv.at[c, k], at_x(x)).wait_recv()

    def partial(c, s):
        return dot(dwt[s], h[c, s].reshape(256, tc))

    def pass_one(c, k, relay):
        s = near[k]
        above = s > yl
        to = jnp.where(above, yl + 1, yl - 1)
        if relay:
            own = partial(c, s)
            remote(rss.at[c, s], rsr.at[c, s], rs_send.at[0], rs_recv.at[c, s], at_line(yl)).wait_recv()
            rss[c, s] = (own + rsr[c, s].astype(F32)).astype(BF16)
        else:
            rss[c, s] = partial(c, s).astype(BF16)
        slot = jnp.where(jnp.logical_and(to == s, above), LINE, s)
        remote(rss.at[c, s], rsr.at[c, slot], rs_send.at[0], rs_recv.at[c, slot], at_line(to)).start()

    def pass_outputs(c, ks, relay):
        @pl.when(interior if relay else jnp.logical_not(interior))
        def _():
            for k in ks:
                pass_one(c, k, relay)

    def end_outputs(c):
        mine = pl.ds(c * tc, tc)
        total = partial(c, yl)

        @pl.when(yl == 0)
        def _():
            remote(rss.at[c, 0], rsr.at[c, 0], rs_send.at[0], rs_recv.at[c, 0], at_line(yl)).wait_recv()
            out_ref[:, mine] = (total + rsr[c, 0].astype(F32)).astype(BF16)

        @pl.when(yl == LINE - 1)
        def _():
            remote(rss.at[c, 0], rsr.at[c, LINE], rs_send.at[0], rs_recv.at[c, LINE], at_line(yl)).wait_recv()
            out_ref[:, mine] = (total + rsr[c, LINE].astype(F32)).astype(BF16)

        @pl.when(interior)
        def _():
            remote(rss.at[c, 0], rsr.at[c, yl], rs_send.at[0], rs_recv.at[c, yl], at_line(yl)).wait_recv()
            remote(rss.at[c, 0], rsr.at[c, LINE], rs_send.at[0], rs_recv.at[c, LINE], at_line(yl)).wait_recv()
            out_ref[:, mine] = (total + rsr[c, yl].astype(F32) + rsr[c, LINE].astype(F32)).astype(BF16)

    def down_term(k):
        row = order[k]
        term = dot_nt(h[0, row].reshape(256, tc), dy[row, 0])
        for c in range(1, chunks):
            term += dot_nt(h[c, row].reshape(256, tc), dy[row, c])
        dacc[k] = term

    def slope_step(c, k):
        wait_back(c, k)
        s = order[k]
        back = g[c, s].reshape(256, tc).astype(F32)
        slope = (back * sf[c, pl.ds(pl.multiple_of(s * 256, 256), 256), :]).astype(BF16)
        g[c, s] = slope.reshape(RING, SUB, tc)
        term = dot_nt(xc[c], slope)
        if c == 0:
            uacc[k] = term
        else:
            uacc[k] += term

    def feature_step(c):
        dx_ref[:, pl.ds(c * tc, tc)] = dot(upv[...], g[c].reshape(1024, tc)).astype(BF16)

    def begin():
        pl.semaphore_wait(barrier, 30 + SHARERS - jnp.where(stays, 2, 0))

    def prepare():
        dw_load.wait()
        dwt[yl] = dw[yl].T
        pltpu.make_async_copy(dy.at[yl], dy.at[yl], load_sem.at[1 + chunks]).wait()

    def prepare_up():
        up_load.wait()
        upt[...] = upv[...].T

    def send_dy(c):
        for way, ok in ((1, yl < LINE - 1), (-1, yl > 0)):

            @pl.when(ok)
            def _():
                remote(
                    dy_hbm.at[:, pl.ds(c * tc, tc)], dy.at[yl, c],
                    ag_send.at[(1 - way) // 2], ag_recv.at[yl, c], at_line(yl + way),
                ).start()

    far = 2 - 4 * core
    share = 256 // (2 * SHARERS)
    mine = pl.ds(pl.multiple_of(part * share, share), share)
    w_copies = []
    for k, delta in enumerate((1, -1, far)):
        to = (y8 + delta + 8) % 8
        rows = pl.ds(pl.multiple_of((to % 4) * 256 + part * share, share), share)
        w_copies.append(
            remote(down_hbm.at[0, rows], dw.at[yl, mine], w_send.at[0], w_recv.at[yl], at_y(delta))
        )

    def send_weights():
        for cp in w_copies:
            cp.start()

    def pass_weights():
        for k in range(1, LINE):
            s = (yl + k) % LINE
            remote(dw.at[s, mine], dw.at[s, mine], w_send.at[0], w_recv.at[s], other_core).wait_recv()
            for n in range(1, 2 * SHARERS):
                to = at_sharer((part + n) % (2 * SHARERS))
                remote(dw.at[s, mine], dw.at[s, mine], w_send.at[0], w2_recv.at[s], to).start()

    def wait_weights():
        for k in range(1, LINE):
            s = (yl + k) % LINE
            got = dw.at[s, pl.ds(0, 256 - share)]
            remote(got, got, w_send.at[0], w2_recv.at[s], other_core).wait_recv()
            dwt[s] = dw[s].T

    def next_hidden(c):
        x_loads[c].wait()
        hidden(c)
        send_hidden(c)

    factor = 1.0 / math.sqrt(tc * chunks * 32)
    other_half = at_y(4)
    groups = []

    def finish_block(kind, k, part):
        part = jnp.concatenate([part[:8], part[8:]], axis=1) * factor
        if kind == "up":
            upg_ref[0, :, pl.ds(pl.multiple_of(order[k] * 256, 256), 256)] = part
            return
        dfin[k] = part
        if k == 0:

            @pl.when(stays)
            def _():
                dgot[pl.ds(pl.multiple_of(piece * 8, 8), 8), :] = part

            pl.when(jnp.logical_not(stays))(lambda: down_copy(0).start())
        else:
            down_copy(k).start()

    def down_copy(k):
        rows = pl.ds(pl.multiple_of(piece * 8, 8), 8)
        return remote(dfin.at[k], dgot.at[rows], df_send.at[0], df_recv.at[0], at_final(order[k]))

    def wait_pieces(count, sent):
        rows = dgot.at[pl.ds(0, 8 * count)]
        copy = remote(rows, rows, df_send.at[0], df_recv.at[0], other_core)
        if sent:
            copy.wait_send()
        else:
            copy.wait_recv()

    def down_end():
        pl.when(stays)(lambda: wait_pieces(3, False))
        pl.when(jnp.logical_not(stays))(lambda: wait_pieces(4, False))
        downg_ref[0] = dgot[...]

    class Group:
        def __init__(self, blocks, refs):
            self.blocks = blocks
            self.direct = len(refs) == 8
            self.split_to, self.got, self.joined, self.parts = refs[:4]
            self.core_sem, self.send, self.recv = refs[4:7]
            self.swap_core = remote(
                self.split_to.at[1 - core], self.got, self.core_sem.at[0], self.core_sem.at[1], other_core
            )
            self.sends = []
            if self.direct:
                for n in range(1, OWNERS):
                    o = (me + n) % OWNERS
                    self.sends.append(
                        remote(self.joined.at[o], self.parts.at[me], self.send.at[0], self.recv.at[0], at_owner(o))
                    )
            else:
                self.total, self.out, self.coming, self.half_sem = refs[7:]
                for n in range(1, Z):
                    zo = (z + n) % Z
                    self.sends.append(
                        remote(
                            self.joined.at[pl.ds(zo * 2, 2)], self.parts.at[z],
                            self.send.at[0], self.recv.at[0], at_owner(zo * 2 + yh),
                        )
                    )
                self.half = remote(
                    self.out.at[1 - yh], self.coming, self.half_sem.at[0], self.half_sem.at[1], other_half
                )

        def split(self):
            def body(o, carry):
                for half in range(2):
                    for n, (kind, k) in enumerate(self.blocks):
                        if kind == "up":
                            part = uacc[k, pl.ds(pl.multiple_of(16 * o + 8 * half, 8), 8), :]
                        else:
                            first = (o // 4) * 64 + half * 32 + (o % 4) * 8
                            part = dacc[k, pl.ds(pl.multiple_of(first, 8), 8), :]
                        self.split_to[half, o, n] = jnp.concatenate([part[:, :128], part[:, 128:]], axis=0).astype(BF16)
                return carry

            lax.fori_loop(0, OWNERS, body, 0)
            self.swap_core.start()

        def join(self):
            self.swap_core.wait()

            def body(o, carry):
                self.joined[o] = (self.split_to[core, o].astype(F32) + self.got[o].astype(F32)).astype(BF16)
                return carry

            lax.fori_loop(0, OWNERS, body, 0)
            for cp in self.sends:
                cp.start()

        def wait_parts(self, count):
            got = self.parts.at[pl.ds(0, count)]
            remote(got, got, self.send.at[0], self.recv.at[0], other_core).wait_recv()

        def wait_sends(self):
            sent = self.parts.at[pl.ds(0, OWNERS - 1 if self.direct else Z - 1)]
            remote(sent, sent, self.send.at[0], self.recv.at[0], other_core).wait_send()

        def sum_z(self):
            add = self.joined[pl.ds(z * 2, 2)].astype(F32)
            self.wait_parts(Z - 1)
            for n in range(1, Z):
                add += self.parts[(z - n + Z) % Z].astype(F32)
            self.total[...] = add
            self.out[...] = add.astype(BF16)
            self.half.start()

        def end(self):
            if self.direct:
                total = self.joined[me].astype(F32)
                self.wait_parts(OWNERS - 1)
                for n in range(1, OWNERS):
                    total += self.parts[(me - n + OWNERS) % OWNERS].astype(F32)
            else:
                self.half.wait()
                total = self.total[yh] + self.coming[...].astype(F32)
            for n, (kind, k) in enumerate(self.blocks):
                finish_block(kind, k, total[n])

    at = 0
    for blocks, direct in GROUPS:
        count = 7 if direct else 11
        refs = list(group_refs[at : at + count])
        at += count
        groups.append(Group(blocks, refs + [None] if direct else refs))

    steps = {
        "begin": begin,
        "prepare": prepare,
        "prepare_up": prepare_up,
        "dy": send_dy,
        "weights": send_weights,
        "weights_pass": pass_weights,
        "weights_in": wait_weights,
        "hidden": next_hidden,
        "hidden_in": wait_hidden,
        "r1": lambda c: pass_outputs(c, (2, 1, 0), False),
        "r2": lambda c: pass_outputs(c, (2, 1), True),
        "r3": lambda c: pass_outputs(c, (0,), True),
        "out": end_outputs,
        "b": lambda c: send_back(c, 0, None),
        "dx": feature_step,
        "down": down_term,
        "down_end": down_end,
    }
    for n, group in enumerate(groups):
        steps[f"split{n}"] = group.split
        steps[f"join{n}"] = group.join
        steps[f"end{n}"] = group.end
        if not group.direct:
            steps[f"sum{n}"] = group.sum_z
    for k in range(1, LINE):
        steps[f"i{k}"] = lambda c, k=k: gather(c, k - 1, interior)
        steps[f"e{k}"] = lambda c, k=k: gather(c, k - 1, edge)
        steps[f"ib{k}"] = lambda c, k=k: send_back(c, k, interior)
        steps[f"eb{k}"] = lambda c, k=k: send_back(c, k, edge)
    for k in range(LINE):
        steps[f"slope{k}"] = lambda c, k=k: slope_step(c, k)
    for name, *at_chunks in PLAN:
        if at_chunks:
            for c in at_chunks:
                steps[name](c)
        else:
            steps[name]()

    def sent(ref, sem):
        remote(ref, ref, sem, sem, other_core).wait_send()

    sent(hs.at[:, :, pl.ds(0, RING - 1)], hs_send.at[0])
    sent(b.at[:, :, pl.ds(0, RING - 1)], b_send.at[0])
    sent(rss.at[:, pl.ds(0, LINE - 1)], rs_send.at[0])
    sent(dw.at[pl.ds(0, LINE - 1)], w_send.at[0])
    for group in groups:
        group.wait_sends()
    pl.when(stays)(lambda: wait_pieces(3, True))
    pl.when(jnp.logical_not(stays))(lambda: wait_pieces(4, True))
    pl.when(yl < LINE - 1)(lambda: sent(dy.at[0], ag_send.at[0]))
    pl.when(yl > 0)(lambda: sent(dy.at[0], ag_send.at[1]))
    pl.when(interior)(lambda: sent(dy.at[pl.ds(0, LINE - 1)], ag_send.at[2]))


def finish(*refs):
    for i in range(4):
        refs[4 + i][...] = refs[i][...]


def on_device(features, cotangent, up_blocks, down_blocks):
    wide, tokens = features.shape
    tc = tokens // CHUNKS
    hidden_units = up_blocks.shape[2]
    vm = pltpu.VMEM
    dma = pltpu.SemaphoreType.DMA
    grid = (CHUNKS, LINE, RING, SUB, tc)
    scratch = [
        vm((CHUNKS, wide, tc), BF16),
        vm((LINE, CHUNKS, wide, tc), BF16),
        vm((wide, hidden_units), BF16),
        vm((hidden_units, wide), BF16),
        vm((LINE, 256, wide), BF16),
        vm((LINE, wide, 256), BF16),
        vm(grid, BF16),
        vm(grid, BF16),
        vm((CHUNKS, hidden_units, tc), F32),
        vm(grid, BF16),
        vm(grid, BF16),
        vm((CHUNKS, LINE, wide, tc), BF16),
        vm((CHUNKS, LINE + 1, wide, tc), BF16),
        vm((LINE, 256, wide), F32),
        vm((LINE, wide, 256), F32),
        vm((LINE, 8, wide), F32),
        vm((32, wide), F32),
        dma((3 + CHUNKS,)),
        dma((1,)), dma((LINE,)), dma((LINE,)),
        dma((3,)), dma((LINE, CHUNKS)),
        dma((1,)), dma((CHUNKS,)),
        dma((1,)), dma((CHUNKS, LINE)),
        dma((1,)), dma((CHUNKS, LINE + 1)),
        dma((1,)), dma((1,)),
    ]
    for blocks, direct in GROUPS:
        n = len(blocks)
        piece = (n, 16, 128)
        scratch += [
            vm((2, OWNERS, *piece), BF16),
            vm((OWNERS, *piece), BF16),
            vm((OWNERS, *piece), BF16),
            vm((OWNERS, *piece) if direct else (Z, 2, *piece), BF16),
            dma((2,)), dma((1,)), dma((1,)),
        ]
        if not direct:
            scratch += [vm((2, *piece), F32), vm((2, *piece), BF16), vm(piece, BF16), dma((2,))]
    vmem = pl.BlockSpec(memory_space=pltpu.VMEM)
    hbm = pl.BlockSpec(memory_space=pltpu.HBM)
    results = pl.pallas_call(
        kernel,
        name="monarch",
        out_shape=(
            jax.ShapeDtypeStruct((wide, tokens), BF16),
            jax.ShapeDtypeStruct((wide, tokens), BF16),
            jax.ShapeDtypeStruct((1, 8, hidden_units), F32),
            jax.ShapeDtypeStruct((1, 32, wide), F32),
        ),
        in_specs=[hbm] * 4,
        out_specs=[vmem] * 4,
        scratch_shapes=scratch,
        compiler_params=pltpu.CompilerParams(
            collective_id=0, has_side_effects=True, vmem_limit_bytes=63 * 2**20
        ),
    )(features, cotangent, up_blocks, down_blocks)
    anywhere = pl.BlockSpec(memory_space=pl.ANY)
    return pl.pallas_call(
        finish,
        name="finish",
        out_shape=tuple(jax.ShapeDtypeStruct(r.shape, r.dtype) for r in results),
        in_specs=[vmem] * 4,
        out_specs=[vmem] * 4,
    )(*results)


def solution(mesh):
    in_specs = (
        P("tensor", "dp"),
        P("tensor", "dp"),
        P("tensor", None, None),
        P("tensor", None, None),
    )
    out_specs = (
        P("tensor", "dp"),
        P("tensor", "dp"),
        P("tensor", "dp", None),
        P("tensor", "dp", None),
    )
    return jax.shard_map(
        on_device, mesh=mesh, in_specs=in_specs, out_specs=out_specs, check_vma=False
    )
```

```python
import math

import jax
import jax.numpy as jnp
from jax import lax
from jax.experimental import pallas as pl
from jax.experimental.pallas import tpu as pltpu
from jax.sharding import PartitionSpec as P

LINE = 4
RING = 4
SUB = 64
CHUNKS = 3
OWNERS = 16
Z = 8
SHARERS = 2

PLAN = (
    ("begin",), ("weights",), ("dy", 0, 1, 2), ("prepare_up",), ("hidden", 0), ("weights_pass",), ("prepare",),
    ("hidden", 1), ("i1", 0), ("i2", 0), ("b", 0, 1, 2), ("hidden", 2), ("weights_in",), ("i1", 1), ("i2", 1),
    ("hidden_in", 0), ("r1", 0), ("i1", 2), ("i2", 2), ("ib1", 0, 1, 2), ("e1", 0), ("eb1", 0), ("e1", 1),
    ("eb1", 1), ("e1", 2), ("eb1", 2), ("i3", 0), ("hidden_in", 1), ("r1", 1), ("i3", 1), ("r2", 0),
    ("ib2", 0, 1, 2), ("i3", 2), ("ib3", 0, 1, 2), ("e2", 0), ("eb2", 0), ("e2", 1), ("eb2", 1), ("e2", 2),
    ("eb2", 2), ("r3", 0), ("hidden_in", 2), ("r1", 2), ("down", 0, 1, 2), ("split0",), ("slope0", 0, 1, 2),
    ("r2", 1), ("join0",), ("slope1", 0, 1, 2), ("e3", 0), ("eb3", 0), ("e3", 1), ("eb3", 1), ("e3", 2),
    ("eb3", 2), ("down", 3), ("split2",), ("r3", 1), ("join2",), ("slope2", 0, 1, 2), ("split1",), ("sum0",),
    ("slope3", 0, 1, 2), ("split3",), ("join1",), ("end0",), ("out", 0), ("r2", 2), ("join3",), ("sum1",),
    ("end2",), ("out", 1), ("r3", 2), ("end1",), ("dx", 0, 1, 2), ("out", 2), ("end3",), ("down_end",),
)
GROUPS = (
    ((("down", 0), ("down", 1), ("down", 2),), False),
    ((("up", 0), ("up", 1), ("up", 2),), False),
    ((("down", 3),), True),
    ((("up", 3),), True),
)

INV_ROOT2 = 0.7071067811865476
INV_ROOT2PI = 0.3989422804014327

BF16 = jnp.bfloat16
F32 = jnp.float32
MESH = pl.DeviceIdType.MESH


def dot(a, b):
    return jnp.dot(a, b, preferred_element_type=F32)


def dot_nt(a, b):
    return lax.dot_general(a, b, (((1,), (1,)), ((), ())), preferred_element_type=F32)


def kernel(
    x_hbm, dy_hbm, up_hbm, down_hbm,
    out_ref, dx_ref, upg_ref, downg_ref,
    xc, dy, upv, upt, dw, dwt, hs, h, sf, b, g, rss, rsr,
    dacc, uacc, dfin, dgot,
    load_sem, w_send, w_recv, w2_recv, ag_send, ag_recv, hs_send, hs_recv, b_send, b_recv,
    rs_send, rs_recv, df_send, df_recv, *group_refs,
):
    chunks, wide, tc = xc.shape
    dp = lax.axis_index("dp")
    tensor = lax.axis_index("tensor")
    z = dp // 4
    yh = (dp // 2) % 2
    core = dp % 2
    yl = tensor // 4
    x = tensor % 4
    y8 = yh * 4 + yl
    me = dp // 2
    interior = jnp.logical_and(yl > 0, yl < LINE - 1)

    def at_y(delta):
        to = (y8 + delta + 8) % 8
        return {"dp": (z * 2 + to // 4) * 2 + core, "tensor": (to % 4) * 4 + x}

    def at_line(to):
        return {"dp": dp, "tensor": to * 4 + x}

    def at_x(to):
        return {"dp": dp, "tensor": yl * 4 + to}

    def at_owner(o):
        return {"dp": o * 2 + core, "tensor": tensor}

    part = (z % SHARERS) * 2 + core

    def at_sharer(p):
        return {"dp": ((z // SHARERS * SHARERS + p // 2) * 2 + yh) * 2 + p % 2, "tensor": tensor}

    other_core = {"dp": dp + 1 - 2 * core, "tensor": tensor}
    final_z = 2 * yl + z // 4
    final_yh = (z // 2) % 2
    stays = jnp.logical_and(final_z == z, final_yh == yh)
    piece = (z % 2) * 2 + yh

    def at_final(row):
        return {"dp": (final_z * 2 + final_yh) * 2 + core, "tensor": row * 4 + x}

    from_y = z // 2
    from_x = (z % 2) * 2 + yh

    def at_source(n):
        return {"dp": ((2 * from_x + n // 2) * 2 + n % 2) * 2 + core, "tensor": from_y * 4 + x}

    def is_self(n):
        same = jnp.logical_and(2 * from_x + n // 2 == z, n % 2 == yh)
        return jnp.logical_and(from_y == yl, same)

    def remote(src, dst, send, recv, where):
        return pltpu.make_async_remote_copy(
            src_ref=src, dst_ref=dst, send_sem=send, recv_sem=recv, device_id=where, device_id_type=MESH
        )

    barrier = pltpu.get_barrier_semaphore()

    def greet(where):
        pl.semaphore_signal(barrier, inc=1, device_id=where, device_id_type=MESH)

    for delta in (1, -1, 2, -2):
        greet(at_y(delta))
    for k in range(1, RING):
        greet(at_x((x + k) % RING))
    greet(other_core)
    for k in range(1, OWNERS):
        greet(at_owner((me + k) % OWNERS))

    for n in range(1, SHARERS):
        greet(at_sharer((part + 2 * n + 1 - 2 * core) % (2 * SHARERS)))
    for k in range(LINE):

        @pl.when(jnp.logical_not(jnp.logical_and(stays, k == yl)))
        def _():
            greet(at_final(k))

        @pl.when(jnp.logical_not(is_self(k)))
        def _():
            greet(at_source(k))

    up_load = pltpu.make_async_copy(up_hbm.at[0], upv, load_sem.at[0])
    up_load.start()
    x_loads = []
    for c in range(chunks):
        cp = pltpu.make_async_copy(x_hbm.at[:, pl.ds(c * tc, tc)], xc.at[c], load_sem.at[1 + c])
        cp.start()
        x_loads.append(cp)
    for c in range(chunks):
        cp = pltpu.make_async_copy(dy_hbm.at[:, pl.ds(c * tc, tc)], dy.at[yl, c], load_sem.at[1 + chunks])
        cp.start()
    dw_load = pltpu.make_async_copy(
        down_hbm.at[0, pl.ds(yl * 256, 256)], dw.at[yl], load_sem.at[2 + chunks]
    )
    dw_load.start()


    def hidden(c):
        def body(k, carry):
            p = dot(upt[pl.ds(k * 256, 256), :], xc[c]).astype(BF16).astype(F32)
            cdf = 0.5 * (1.0 + lax.erf(p * INV_ROOT2))
            hs[c, k] = (p * cdf).astype(BF16).reshape(RING, SUB, tc)
            sf[c, pl.ds(k * 256, 256), :] = cdf + p * jnp.exp(-0.5 * p * p) * INV_ROOT2PI
            return carry

        lax.fori_loop(0, LINE, body, 0)

    def send_hidden(c):
        for k in range(1, RING):
            to = (x + k) % RING
            cp = remote(hs.at[c, :, to], h.at[c, :, x], hs_send.at[0], hs_recv.at[c], at_x(to))
            cp.start()
        h[c, :, x] = hs[c, :, x]

    def wait_hidden(c):
        got = h.at[c, :, pl.ds(0, RING - 1)]
        remote(got, got, hs_send.at[0], hs_recv.at[c], at_x(x)).wait_recv()

    near = [yl + 1 - 2 * (yl % 2), 2 - yl // 2, 3 - 3 * (yl // 2)]

    edge = jnp.logical_not(interior)

    def gather(c, k, role):
        s = near[k]
        to = jnp.where(s > yl, yl - 1, yl + 1)

        @pl.when(role)
        def _():
            cp = remote(dy.at[s, c], dy.at[s, c], ag_send.at[2], ag_recv.at[s, c], at_line(to))
            cp.wait_recv()
            if role is interior:
                cp.start()

    order = [yl] + near

    def back_sends(c, k):
        s = order[k]
        copies = []
        for n in range(1, RING):
            to = (x + n) % RING
            copies.append(
                remote(b.at[c, s, to], g.at[c, s, x], b_send.at[0], b_recv.at[c, k], at_x(to))
            )
        return copies

    def send_back(c, k, role):
        def run():
            s = order[k]
            b[c, s] = dot(dw[s], dy[s, c]).astype(BF16).reshape(RING, SUB, tc)
            for cp in back_sends(c, k):
                cp.start()
            g[c, s, x] = b[c, s, x]

        if role is None:
            run()
        else:
            pl.when(role)(run)

    def wait_back(c, k):
        got = g.at[c, order[k], pl.ds(0, RING - 1)]
        remote(got, got, b_send.at[0], b_recv.at[c, k], at_x(x)).wait_recv()

    def partial(c, s):
        return dot(dwt[s], h[c, s].reshape(256, tc))

    def pass_one(c, k, relay):
        s = near[k]
        above = s > yl
        to = jnp.where(above, yl + 1, yl - 1)
        if relay:
            own = partial(c, s)
            remote(rss.at[c, s], rsr.at[c, s], rs_send.at[0], rs_recv.at[c, s], at_line(yl)).wait_recv()
            rss[c, s] = (own + rsr[c, s].astype(F32)).astype(BF16)
        else:
            rss[c, s] = partial(c, s).astype(BF16)
        slot = jnp.where(jnp.logical_and(to == s, above), LINE, s)
        remote(rss.at[c, s], rsr.at[c, slot], rs_send.at[0], rs_recv.at[c, slot], at_line(to)).start()

    def pass_outputs(c, ks, relay):
        @pl.when(interior if relay else jnp.logical_not(interior))
        def _():
            for k in ks:
                pass_one(c, k, relay)

    def end_outputs(c):
        mine = pl.ds(c * tc, tc)
        total = partial(c, yl)

        @pl.when(yl == 0)
        def _():
            remote(rss.at[c, 0], rsr.at[c, 0], rs_send.at[0], rs_recv.at[c, 0], at_line(yl)).wait_recv()
            out_ref[:, mine] = (total + rsr[c, 0].astype(F32)).astype(BF16)

        @pl.when(yl == LINE - 1)
        def _():
            remote(rss.at[c, 0], rsr.at[c, LINE], rs_send.at[0], rs_recv.at[c, LINE], at_line(yl)).wait_recv()
            out_ref[:, mine] = (total + rsr[c, LINE].astype(F32)).astype(BF16)

        @pl.when(interior)
        def _():
            remote(rss.at[c, 0], rsr.at[c, yl], rs_send.at[0], rs_recv.at[c, yl], at_line(yl)).wait_recv()
            remote(rss.at[c, 0], rsr.at[c, LINE], rs_send.at[0], rs_recv.at[c, LINE], at_line(yl)).wait_recv()
            out_ref[:, mine] = (total + rsr[c, yl].astype(F32) + rsr[c, LINE].astype(F32)).astype(BF16)

    def down_term(k):
        row = order[k]
        term = dot_nt(h[0, row].reshape(256, tc), dy[row, 0])
        for c in range(1, chunks):
            term += dot_nt(h[c, row].reshape(256, tc), dy[row, c])
        dacc[k] = term

    def slope_step(c, k):
        wait_back(c, k)
        s = order[k]
        back = g[c, s].reshape(256, tc).astype(F32)
        slope = (back * sf[c, pl.ds(pl.multiple_of(s * 256, 256), 256), :]).astype(BF16)
        g[c, s] = slope.reshape(RING, SUB, tc)
        term = dot_nt(xc[c], slope)
        if c == 0:
            uacc[k] = term
        else:
            uacc[k] += term

    def feature_step(c):
        dx_ref[:, pl.ds(c * tc, tc)] = dot(upv[...], g[c].reshape(1024, tc)).astype(BF16)

    def begin():
        pl.semaphore_wait(barrier, 30 + SHARERS - jnp.where(stays, 2, 0))

    def prepare():
        dw_load.wait()
        dwt[yl] = dw[yl].T
        pltpu.make_async_copy(dy.at[yl], dy.at[yl], load_sem.at[1 + chunks]).wait()

    def prepare_up():
        up_load.wait()
        upt[...] = upv[...].T

    def send_dy(c):
        for way, ok in ((1, yl < LINE - 1), (-1, yl > 0)):

            @pl.when(ok)
            def _():
                remote(
                    dy_hbm.at[:, pl.ds(c * tc, tc)], dy.at[yl, c],
                    ag_send.at[(1 - way) // 2], ag_recv.at[yl, c], at_line(yl + way),
                ).start()

    far = 2 - 4 * core
    share = 256 // (2 * SHARERS)
    mine = pl.ds(pl.multiple_of(part * share, share), share)
    w_copies = []
    for k, delta in enumerate((1, -1, far)):
        to = (y8 + delta + 8) % 8
        rows = pl.ds(pl.multiple_of((to % 4) * 256 + part * share, share), share)
        w_copies.append(
            remote(down_hbm.at[0, rows], dw.at[yl, mine], w_send.at[0], w_recv.at[yl], at_y(delta))
        )

    def send_weights():
        for cp in w_copies:
            cp.start()

    def pass_weights():
        for k in range(1, LINE):
            s = (yl + k) % LINE
            remote(dw.at[s, mine], dw.at[s, mine], w_send.at[0], w_recv.at[s], other_core).wait_recv()
            for n in range(1, 2 * SHARERS):
                to = at_sharer((part + n) % (2 * SHARERS))
                remote(dw.at[s, mine], dw.at[s, mine], w_send.at[0], w2_recv.at[s], to).start()

    def wait_weights():
        for k in range(1, LINE):
            s = (yl + k) % LINE
            got = dw.at[s, pl.ds(0, 256 - share)]
            remote(got, got, w_send.at[0], w2_recv.at[s], other_core).wait_recv()
            dwt[s] = dw[s].T

    def next_hidden(c):
        x_loads[c].wait()
        hidden(c)
        send_hidden(c)

    factor = 1.0 / math.sqrt(tc * chunks * 32)
    other_half = at_y(4)
    groups = []

    def finish_block(kind, k, part):
        part = jnp.concatenate([part[:8], part[8:]], axis=1) * factor
        if kind == "up":
            upg_ref[0, :, pl.ds(pl.multiple_of(order[k] * 256, 256), 256)] = part
            return
        dfin[k] = part
        if k == 0:

            @pl.when(stays)
            def _():
                dgot[pl.ds(pl.multiple_of(piece * 8, 8), 8), :] = part

            pl.when(jnp.logical_not(stays))(lambda: down_copy(0).start())
        else:
            down_copy(k).start()

    def down_copy(k):
        rows = pl.ds(pl.multiple_of(piece * 8, 8), 8)
        return remote(dfin.at[k], dgot.at[rows], df_send.at[0], df_recv.at[0], at_final(order[k]))

    def wait_pieces(count, sent):
        rows = dgot.at[pl.ds(0, 8 * count)]
        copy = remote(rows, rows, df_send.at[0], df_recv.at[0], other_core)
        if sent:
            copy.wait_send()
        else:
            copy.wait_recv()

    def down_end():
        pl.when(stays)(lambda: wait_pieces(3, False))
        pl.when(jnp.logical_not(stays))(lambda: wait_pieces(4, False))
        downg_ref[0] = dgot[...]

    class Group:
        def __init__(self, blocks, refs):
            self.blocks = blocks
            self.direct = len(refs) == 8
            self.split_to, self.got, self.joined, self.parts = refs[:4]
            self.core_sem, self.send, self.recv = refs[4:7]
            self.swap_core = remote(
                self.split_to.at[1 - core], self.got, self.core_sem.at[0], self.core_sem.at[1], other_core
            )
            self.sends = []
            if self.direct:
                for n in range(1, OWNERS):
                    o = (me + n) % OWNERS
                    self.sends.append(
                        remote(self.joined.at[o], self.parts.at[me], self.send.at[0], self.recv.at[0], at_owner(o))
                    )
            else:
                self.total, self.out, self.coming, self.half_sem = refs[7:]
                for n in range(1, Z):
                    zo = (z + n) % Z
                    self.sends.append(
                        remote(
                            self.joined.at[pl.ds(zo * 2, 2)], self.parts.at[z],
                            self.send.at[0], self.recv.at[0], at_owner(zo * 2 + yh),
                        )
                    )
                self.half = remote(
                    self.out.at[1 - yh], self.coming, self.half_sem.at[0], self.half_sem.at[1], other_half
                )

        def split(self):
            def body(o, carry):
                for half in range(2):
                    for n, (kind, k) in enumerate(self.blocks):
                        if kind == "up":
                            part = uacc[k, pl.ds(pl.multiple_of(16 * o + 8 * half, 8), 8), :]
                        else:
                            first = (o // 4) * 64 + half * 32 + (o % 4) * 8
                            part = dacc[k, pl.ds(pl.multiple_of(first, 8), 8), :]
                        self.split_to[half, o, n] = jnp.concatenate([part[:, :128], part[:, 128:]], axis=0).astype(BF16)
                return carry

            lax.fori_loop(0, OWNERS, body, 0)
            self.swap_core.start()

        def join(self):
            self.swap_core.wait()

            def body(o, carry):
                self.joined[o] = (self.split_to[core, o].astype(F32) + self.got[o].astype(F32)).astype(BF16)
                return carry

            lax.fori_loop(0, OWNERS, body, 0)
            for cp in self.sends:
                cp.start()

        def wait_parts(self, count):
            got = self.parts.at[pl.ds(0, count)]
            remote(got, got, self.send.at[0], self.recv.at[0], other_core).wait_recv()

        def wait_sends(self):
            sent = self.parts.at[pl.ds(0, OWNERS - 1 if self.direct else Z - 1)]
            remote(sent, sent, self.send.at[0], self.recv.at[0], other_core).wait_send()

        def sum_z(self):
            add = self.joined[pl.ds(z * 2, 2)].astype(F32)
            self.wait_parts(Z - 1)
            for n in range(1, Z):
                add += self.parts[(z - n + Z) % Z].astype(F32)
            self.total[...] = add
            self.out[...] = add.astype(BF16)
            self.half.start()

        def end(self):
            if self.direct:
                total = self.joined[me].astype(F32)
                self.wait_parts(OWNERS - 1)
                for n in range(1, OWNERS):
                    total += self.parts[(me - n + OWNERS) % OWNERS].astype(F32)
            else:
                self.half.wait()
                total = self.total[yh] + self.coming[...].astype(F32)
            for n, (kind, k) in enumerate(self.blocks):
                finish_block(kind, k, total[n])

    at = 0
    for blocks, direct in GROUPS:
        count = 7 if direct else 11
        refs = list(group_refs[at : at + count])
        at += count
        groups.append(Group(blocks, refs + [None] if direct else refs))

    steps = {
        "begin": begin,
        "prepare": prepare,
        "prepare_up": prepare_up,
        "dy": send_dy,
        "weights": send_weights,
        "weights_pass": pass_weights,
        "weights_in": wait_weights,
        "hidden": next_hidden,
        "hidden_in": wait_hidden,
        "r1": lambda c: pass_outputs(c, (2, 1, 0), False),
        "r2": lambda c: pass_outputs(c, (2, 1), True),
        "r3": lambda c: pass_outputs(c, (0,), True),
        "out": end_outputs,
        "b": lambda c: send_back(c, 0, None),
        "dx": feature_step,
        "down": down_term,
        "down_end": down_end,
    }
    for n, group in enumerate(groups):
        steps[f"split{n}"] = group.split
        steps[f"join{n}"] = group.join
        steps[f"end{n}"] = group.end
        if not group.direct:
            steps[f"sum{n}"] = group.sum_z
    for k in range(1, LINE):
        steps[f"i{k}"] = lambda c, k=k: gather(c, k - 1, interior)
        steps[f"e{k}"] = lambda c, k=k: gather(c, k - 1, edge)
        steps[f"ib{k}"] = lambda c, k=k: send_back(c, k, interior)
        steps[f"eb{k}"] = lambda c, k=k: send_back(c, k, edge)
    for k in range(LINE):
        steps[f"slope{k}"] = lambda c, k=k: slope_step(c, k)
    for name, *at_chunks in PLAN:
        if at_chunks:
            for c in at_chunks:
                steps[name](c)
        else:
            steps[name]()

    def sent(ref, sem):
        remote(ref, ref, sem, sem, other_core).wait_send()

    sent(hs.at[:, :, pl.ds(0, RING - 1)], hs_send.at[0])
    sent(b.at[:, :, pl.ds(0, RING - 1)], b_send.at[0])
    sent(rss.at[:, pl.ds(0, LINE - 1)], rs_send.at[0])
    sent(dw.at[pl.ds(0, LINE - 1)], w_send.at[0])
    for group in groups:
        group.wait_sends()
    pl.when(stays)(lambda: wait_pieces(3, True))
    pl.when(jnp.logical_not(stays))(lambda: wait_pieces(4, True))
    pl.when(yl < LINE - 1)(lambda: sent(dy.at[0], ag_send.at[0]))
    pl.when(yl > 0)(lambda: sent(dy.at[0], ag_send.at[1]))
    pl.when(interior)(lambda: sent(dy.at[pl.ds(0, LINE - 1)], ag_send.at[2]))


def finish(*refs):
    for i in range(4):
        refs[4 + i][...] = refs[i][...]


def on_device(features, cotangent, up_blocks, down_blocks):
    wide, tokens = features.shape
    tc = tokens // CHUNKS
    hidden_units = up_blocks.shape[2]
    vm = pltpu.VMEM
    dma = pltpu.SemaphoreType.DMA
    grid = (CHUNKS, LINE, RING, SUB, tc)
    scratch = [
        vm((CHUNKS, wide, tc), BF16),
        vm((LINE, CHUNKS, wide, tc), BF16),
        vm((wide, hidden_units), BF16),
        vm((hidden_units, wide), BF16),
        vm((LINE, 256, wide), BF16),
        vm((LINE, wide, 256), BF16),
        vm(grid, BF16),
        vm(grid, BF16),
        vm((CHUNKS, hidden_units, tc), F32),
        vm(grid, BF16),
        vm(grid, BF16),
        vm((CHUNKS, LINE, wide, tc), BF16),
        vm((CHUNKS, LINE + 1, wide, tc), BF16),
        vm((LINE, 256, wide), F32),
        vm((LINE, wide, 256), F32),
        vm((LINE, 8, wide), F32),
        vm((32, wide), F32),
        dma((3 + CHUNKS,)),
        dma((1,)), dma((LINE,)), dma((LINE,)),
        dma((3,)), dma((LINE, CHUNKS)),
        dma((1,)), dma((CHUNKS,)),
        dma((1,)), dma((CHUNKS, LINE)),
        dma((1,)), dma((CHUNKS, LINE + 1)),
        dma((1,)), dma((1,)),
    ]
    for blocks, direct in GROUPS:
        n = len(blocks)
        piece = (n, 16, 128)
        scratch += [
            vm((2, OWNERS, *piece), BF16),
            vm((OWNERS, *piece), BF16),
            vm((OWNERS, *piece), BF16),
            vm((OWNERS, *piece) if direct else (Z, 2, *piece), BF16),
            dma((2,)), dma((1,)), dma((1,)),
        ]
        if not direct:
            scratch += [vm((2, *piece), F32), vm((2, *piece), BF16), vm(piece, BF16), dma((2,))]
    vmem = pl.BlockSpec(memory_space=pltpu.VMEM)
    hbm = pl.BlockSpec(memory_space=pltpu.HBM)
    results = pl.pallas_call(
        kernel,
        name="monarch",
        out_shape=(
            jax.ShapeDtypeStruct((wide, tokens), BF16),
            jax.ShapeDtypeStruct((wide, tokens), BF16),
            jax.ShapeDtypeStruct((1, 8, hidden_units), F32),
            jax.ShapeDtypeStruct((1, 32, wide), F32),
        ),
        in_specs=[hbm] * 4,
        out_specs=[vmem] * 4,
        scratch_shapes=scratch,
        compiler_params=pltpu.CompilerParams(
            collective_id=0, has_side_effects=True, vmem_limit_bytes=63 * 2**20
        ),
    )(features, cotangent, up_blocks, down_blocks)
    columns = pl.BlockSpec((wide, tokens // 2), lambda i: (0, i))
    blocks_of = [
        columns,
        columns,
        pl.BlockSpec((1, 8, hidden_units // 2), lambda i: (0, 0, i)),
        pl.BlockSpec((1, 32, wide // 2), lambda i: (0, 0, i)),
    ]
    return pl.pallas_call(
        finish,
        name="finish",
        out_shape=tuple(jax.ShapeDtypeStruct(r.shape, r.dtype) for r in results),
        grid=(2,),
        in_specs=blocks_of,
        out_specs=blocks_of,
    )(*results)


def solution(mesh):
    in_specs = (
        P("tensor", "dp"),
        P("tensor", "dp"),
        P("tensor", None, None),
        P("tensor", None, None),
    )
    out_specs = (
        P("tensor", "dp"),
        P("tensor", "dp"),
        P("tensor", "dp", None),
        P("tensor", "dp", None),
    )
    return jax.shard_map(
        on_device, mesh=mesh, in_specs=in_specs, out_specs=out_specs, check_vma=False
    )
```
